32 devices in a mesh: sec: 2 (over y), sp: 4 (over x, core), dp: 4 (over z).
Axes of the slice: x: 2, y: 2, z: 4, core: 2. Of those that a mesh axis runs over, the one named last changes fastest.
Arguments:
- fraction: float32 [4, 8, 32, 1024], P('dp', None, 'sp', 'sec'), may hold values from 0 to 1
- labels: int32 [4, 8, 32, 1024], P('dp', ('sec', 'sp')), may hold values from 0 to 63
- conv_weight: bfloat16 [54, 64], replicated, may hold values from -6 to 6
- conv_bias: float32 [64], replicated, may hold values from -6 to 6
- out_weight: bfloat16 [64, 64], replicated, may hold values from -6 to 6
- out_bias: float32 [64], replicated, may hold values from -6 to 6
Outputs:
- cell_loss: float32 [4, 8, 32, 1024], P('dp', ('sec', 'sp'))
- conv_weight_grad: float32 [54, 64], replicated
- conv_bias_grad: float32 [64], replicated
- out_weight_grad: float32 [64, 64], replicated
- out_bias_grad: float32 [64], replicated
The draws below stay inside these ranges and needn't reach their ends.
All inputs are finite; a program needn't handle non-finite values.
Results may differ from the reference program's by a relative error of at most 0.00035.
The reference program's roundings to bfloat16 on the way (of `features`, `columns`, `hidden_act`, `residual_low` and `hidden_low`) count: a program that leaves them out, or rounds other values in their place, can miss the bound.
Values may be sent and summed in bfloat16 or wider, within the bound.
No kernel may reach another device: no remote copies, remote signals or barrier semaphores. Data moves between devices by JAX's collectives and lax.ppermute only.
A program may use at most 64 MiB of HBM per device.

```python
import jax
import jax.numpy as jnp
from jax import lax

PX = 32
PY = 32
PZ = 32
HID = 64
BINS = 64
GROUPS = 4
GP = 8
PLANE = 1024
FEATS = 54
CELLS_ALL = 1048576


def plant(array, key, least, top_value):
    longest = array.shape.index(max(array.shape))
    spots = []
    for shift in (0, 1):
        where = [jax.random.randint(jax.random.fold_in(key, axis), (), 0, length) for axis, length in enumerate(array.shape)]
        where[longest] = (where[longest] + shift) % array.shape[longest]
        spots.append(tuple(where))
    return array.at[spots[0]].set(least).at[spots[1]].set(top_value)


def levels(stream_key, extent, pieces, low, largest):
    level, own = 1.0, jax.random.fold_in(stream_key, 6)
    for dim, parts in pieces:
        heights = jnp.exp(jax.random.uniform(jax.random.fold_in(own, dim), (parts,), jnp.float32, low / len(pieces), largest / len(pieces)))
        level = level * jnp.repeat(heights, extent[dim] // parts).reshape([-1 if axis == dim else 1 for axis in range(len(extent))])
    return level


def normal_values(rng, dims, scale, reach, held_as=jnp.bfloat16):
    return jnp.clip(scale * jax.random.normal(rng, dims, jnp.float32), -reach, reach).astype(held_as)


def setup_inputs(seed: int = 0) -> dict:
    splits = jax.random.split(jax.random.key(seed), 7)
    return {
        "fraction": jnp.clip(1.0 * jax.random.uniform(splits[0], (GROUPS, GP, PX, PLANE), jnp.float32) ** levels(splits[0], (GROUPS, GP, PX, PLANE), ((0, 4), (2, 4), (3, 2)), -0.2, 0.2), 0.0, 1.0),
        "labels": plant(jax.random.randint(splits[1], (GROUPS, GP, PX, PLANE), 0, BINS), jax.random.fold_in(splits[1], 1), 0, BINS - 1).astype(jnp.int32),
        "conv_weight": normal_values(splits[2], (FEATS, HID), 0.5, 6.0),
        "conv_bias": normal_values(splits[3], (HID,), 1.0, 6.0, jnp.float32),
        "out_weight": normal_values(splits[4], (HID, BINS), 0.4, 6.0),
        "out_bias": normal_values(splits[5], (BINS,), 1.0, 6.0, jnp.float32),
    }


def shift_cells(values, offset, step_y, step_z):
    length = values.shape[-1]
    margin = PY * PZ + PZ + 1
    widths = [(0, 0)] * (values.ndim - 1) + [(margin, margin)]
    padded = jnp.pad(values, widths)
    shifted = lax.slice_in_dim(padded, margin + offset, margin + offset + length, axis=values.ndim - 1)
    position = jnp.arange(length, dtype=jnp.int32)
    row_y = (position // PZ) % PY + step_y
    col_z = position % PZ + step_z
    inside = (row_y >= 0) & (row_y < PY) & (col_z >= 0) & (col_z < PZ)
    return jnp.where(inside, shifted, jnp.zeros((), values.dtype))


def box_filter(padded):
    x_sums = padded[..., :-2, :] + padded[..., 1:-1, :] + padded[..., 2:, :]
    window_sum = jnp.zeros_like(x_sums)
    for step_y in (-1, 0, 1):
        for step_z in (-1, 0, 1):
            window_sum = window_sum + shift_cells(x_sums, step_y * PZ + step_z, step_y, step_z)
    return window_sum / 27.0


def make_columns(features):
    shifted_list = []
    for step_x in (-1, 0, 1):
        for step_y in (-1, 0, 1):
            for step_z in (-1, 0, 1):
                offset = step_x * PY * PZ + step_y * PZ + step_z
                shifted_list.append(shift_cells(features, offset, step_y, step_z))
    stacked = jnp.stack(shifted_list)
    return stacked.reshape(2 * stacked.shape[0], stacked.shape[2])


def patch_step(features, patch_labels, conv_weight, conv_bias, out_weight, out_bias, weight_scale):
    columns = make_columns(features)
    columns_wide = columns.astype(jnp.float32)
    hidden_pre = jnp.einsum("kc,kh->hc", columns_wide, conv_weight.astype(jnp.float32)) + conv_bias[:, None]
    hidden_act = lax.optimization_barrier(jax.nn.silu(hidden_pre).astype(jnp.bfloat16))
    act_wide = hidden_act.astype(jnp.float32)
    logits = jnp.einsum("hb,hc->bc", out_weight.astype(jnp.float32), act_wide) + out_bias[:, None]
    exp_logits = jnp.exp(logits)
    partition = jnp.sum(exp_logits, axis=0)
    bin_ids = jnp.arange(logits.shape[0], dtype=jnp.int32)[:, None]
    is_label = bin_ids == patch_labels[None, :]
    cell_term = jnp.log(partition) - jnp.sum(jnp.where(is_label, logits, jnp.zeros((), logits.dtype)), axis=0)
    residual = (exp_logits / partition - is_label.astype(jnp.float32)) * weight_scale
    residual_low = lax.optimization_barrier(residual.astype(jnp.bfloat16)).astype(jnp.float32)
    out_weight_grad = jnp.einsum("hc,bc->hb", act_wide, residual_low)
    out_bias_grad = jnp.sum(residual, axis=1)
    hidden_back = jnp.einsum("hb,bc->hc", out_weight.astype(jnp.float32), residual_low)
    sigmoid_pre = jax.nn.sigmoid(hidden_pre)
    hidden_grad = hidden_back * sigmoid_pre * (1.0 + hidden_pre * (1.0 - sigmoid_pre))
    conv_bias_grad = jnp.sum(hidden_grad, axis=1)
    hidden_low = lax.optimization_barrier(hidden_grad.astype(jnp.bfloat16)).astype(jnp.float32)
    conv_weight_grad = jnp.einsum("kc,hc->kh", columns_wide, hidden_low)
    return cell_term, (conv_weight_grad, conv_bias_grad, out_weight_grad, out_bias_grad)


def reference(fraction, labels, conv_weight, conv_bias, out_weight, out_bias):
    patches = fraction.reshape(-1, PX, PY * PZ)
    moments = jnp.stack([patches, patches * patches])
    padded = jnp.pad(moments, ((0, 0), (0, 0), (1, 1), (0, 0)))
    filtered = box_filter(padded)
    mean_part = filtered[0]
    spread = filtered[1] - mean_part * mean_part
    features = lax.optimization_barrier(jnp.stack([mean_part, spread], axis=1).astype(jnp.bfloat16))
    features = features.reshape(features.shape[0], 2, PX * PY * PZ)
    flat_labels = labels.reshape(-1, PX * PY * PZ)
    weight_scale = 1.0 / CELLS_ALL
    initial = (jnp.zeros((FEATS, HID), jnp.float32), jnp.zeros((HID,), jnp.float32),
               jnp.zeros((HID, BINS), jnp.float32), jnp.zeros((BINS,), jnp.float32))

    def accumulate(running, patch_item):
        cell_term, terms = patch_step(patch_item[0], patch_item[1], conv_weight, conv_bias,
                                      out_weight, out_bias, weight_scale)
        return tuple(left + right for left, right in zip(running, terms)), cell_term

    totals, losses = lax.scan(accumulate, initial, (features, flat_labels))
    cell_loss = losses.reshape(labels.shape)
    return (cell_loss, totals[0], totals[1], totals[2], totals[3])
```

```python
import functools

import jax
import jax.numpy as jnp
from jax import lax
from jax.experimental import pallas as pl
from jax.experimental.pallas import tpu as pltpu
from jax.sharding import PartitionSpec as P

PZ = 32
TAPS_X = 3
OFFSETS = 9
WINDOW = 8
GROUP = 4
LANES = 512
SLOTS = 4


def rolled(values, step, axis):
    size = values.shape[axis]
    return pltpu.roll(values, (-step) % size, axis)


def neighbour(values, step, axis, inside):
    return jnp.where(inside, rolled(values, step, axis), 0.0)


def window_rows(cells):
    planes, plane = cells.shape
    plane_x = lax.broadcasted_iota(jnp.int32, cells.shape, 0)
    lane = lax.broadcasted_iota(jnp.int32, cells.shape, 1)
    col_z = lane & (PZ - 1)
    has = {
        (0, -1): plane_x > 0,
        (0, 1): plane_x < planes - 1,
        (PZ, -1): lane >= PZ,
        (PZ, 1): lane < plane - PZ,
        (1, -1): col_z > 0,
        (1, 1): col_z < PZ - 1,
    }

    def box(values):
        for stride in (0, PZ, 1):
            axis = 1 if stride else 0
            step = stride or 1
            values = (
                neighbour(values, -step, axis, has[stride, -1])
                + values
                + neighbour(values, step, axis, has[stride, 1])
            )
        return values * (1.0 / 27.0)

    filt = box(cells)
    spread = box(cells * cells) - filt * filt
    channels = (filt, spread)
    place = plane_x & (WINDOW - 1)
    unused = (place == 0) | (place == WINDOW - 1)
    for side, (step, inside) in enumerate(((-2, plane_x >= 2), (2, plane_x < planes - 2))):
        pair = [jnp.where(unused, 1.0, neighbour(v, step, 0, inside)) for v in channels]
        for k in range(planes // WINDOW):
            rows = [v[k * WINDOW : (k + 1) * WINDOW] for v in pair]
            yield 2 * k + side, jnp.concatenate(rows, axis=0).astype(jnp.bfloat16)


def neighbour_rows(offset):
    return slice(offset * 2 * WINDOW, (offset + 1) * 2 * WINDOW)


def spread_window(window_ref, offset):
    both = window_ref[neighbour_rows(OFFSETS // 2), :]
    step_y, step_z = offset // 3 - 1, offset % 3 - 1
    lane = lax.broadcasted_iota(jnp.int32, both.shape, 1)
    row_y, col_z = lane + step_y * PZ, (lane & (PZ - 1)) + step_z
    inside = (row_y >= 0) & (row_y < both.shape[1]) & (col_z >= 0) & (col_z < PZ)
    values = rolled(both, step_y * PZ + step_z, 1)
    window_ref[neighbour_rows(offset), :] = jnp.where(inside, values, jnp.zeros((), both.dtype))


def contract_cells(left, right):
    return lax.dot_general(
        left, right, (((1,), (1,)), ((), ())), preferred_element_type=jnp.float32
    )


def fold_lanes(values):
    parts = [values[:, i : i + 128] for i in range(0, values.shape[1], 128)]
    return functools.reduce(jnp.add, parts)


def inverse(values):
    rough = pltpu.reciprocal(values, approx=True)
    return rough * (2.0 - values * rough)


def train_patch(
    scale, arrived_ref, labels_ref, conv_ref, out_t_ref, out_ref, loss_ref, grads_ref,
    windows, acts, slopes, residuals, hidden_low, conv_acc, out_acc, conv_bias_acc, out_bias_acc,
    sums, picked, losses, turned_ref, loss_sems,
):
    planes, plane = labels_ref.shape
    taps = conv_ref.shape[1]
    hidden, bins = out_ref.shape
    across = plane // LANES
    tiles = planes // GROUP * across
    cells = jnp.concatenate([arrived_ref[s] for s in range(arrived_ref.shape[0])], axis=1)
    for window, both in window_rows(cells):
        windows[window][neighbour_rows(OFFSETS // 2), :] = both
    beside = [offset for offset in range(OFFSETS) if offset != OFFSETS // 2]
    for offset in beside:
        spread_window(windows[0], offset)
    for ref in (conv_acc, out_acc, conv_bias_acc, out_bias_acc):
        ref[...] = jnp.zeros_like(ref)
    for refs in acts:
        for ref in refs:
            ref[hidden:, :] = jnp.ones((ref.shape[0] - hidden, LANES), jnp.bfloat16)
    bin_ids = lax.broadcasted_iota(jnp.int32, (bins, LANES), 0)

    def place(n):
        return n // across, pl.ds(n % across * LANES, LANES)

    def finish_losses(block):
        rows = pl.ds(block * 8, 8)
        losses[rows, :] = jnp.log(sums[rows, :]) - picked[rows, :]
        return pltpu.make_async_copy(losses.at[rows, :], loss_ref.at[rows, :], loss_sems.at[block])

    def dot(left, right):
        return jnp.dot(left, right, preferred_element_type=jnp.float32)

    def convolve(n, q):
        window, lanes = place(n)
        return dot(conv_ref[q * hidden : (q + 1) * hidden, :], windows[window][:, lanes])

    def products(n, slot, q, back, soft, act):
        return (
            dot(out_ref[...], residuals[(slot - 2) % SLOTS][q][...]) if back else None,
            dot(out_t_ref[...], acts[(slot - 1) % SLOTS][q][...]) if soft else None,
            convolve(n, q) if act else None,
        )

    def project_grad(slot):
        slot = (slot - 3) % SLOTS
        return contract_cells(
            jnp.concatenate([ref[:hidden, :] for ref in acts[slot]], axis=1),
            jnp.concatenate([ref[...] for ref in residuals[slot]], axis=1),
        )

    def convolve_grad(n, slot):
        window, lanes = place(n - 3)
        return contract_cells(
            windows[window][:, lanes],
            jnp.concatenate([ref[...] for ref in hidden_low[(slot - 3) % SLOTS]], axis=0),
        )

    def unactivate(slot, q, back):
        slot = (slot - 2) % SLOTS
        hidden_grad = back * slopes[slot][q][...]
        hidden_low[slot][q][...] = hidden_grad.astype(jnp.bfloat16)
        return fold_lanes(hidden_grad)

    def soften(n, slot, q, logits):
        window, lanes = place(n - 1)
        row = pl.ds(window * GROUP + q, 1)
        exp_logits = jnp.exp(logits)
        partition = jnp.sum(exp_logits, axis=0, keepdims=True)
        is_label = bin_ids == labels_ref[row, lanes]
        sums[row, lanes] = partition
        picked[row, lanes] = jnp.sum(jnp.where(is_label, logits, 0.0), axis=0, keepdims=True)
        residual = exp_logits * (scale * inverse(partition)) - jnp.where(is_label, scale, 0.0)
        residuals[(slot - 1) % SLOTS][q][...] = residual.astype(jnp.bfloat16)
        return fold_lanes(residual)

    def activate(slot, q, half):
        tanh = jnp.tanh(half)
        upper = 1.0 + tanh
        act = half * upper
        acts[slot % SLOTS][q][:hidden, :] = act.astype(jnp.bfloat16)
        slopes[slot % SLOTS][q][...] = upper + act * (1.0 - tanh)

    def has(n):
        return 0 <= n < tiles

    def issue(n, q):
        return products(n, n, q, has(n - 2), has(n - 1), has(n))

    def run(count):
        ahead = issue(0, 0)
        copies = []
        share = pl.cdiv(len(beside), across * GROUP)
        for n in range(count):
            conv_bias, out_bias, out_grad, conv_grad = [], [], None, None
            for q in range(GROUP):
                back, logits, half = ahead
                if n // across + 1 < len(windows):
                    first = (n % across * GROUP + q) * share
                    for offset in beside[first : first + share]:
                        spread_window(windows[n // across + 1], offset)
                ahead = issue(n, q + 1) if q + 1 < GROUP else issue(n + 1, 0)
                if q == 0 and has(n - 3):
                    out_grad = project_grad(n)
                if q == 1 and has(n - 3):
                    conv_grad = convolve_grad(n, n)
                if back is not None:
                    conv_bias.append(unactivate(n, q, back))
                if logits is not None:
                    out_bias.append(soften(n, n, q, logits))
                if half is not None:
                    activate(n, q, half)
            if has(n - 3):
                out_acc[...] += out_grad
                conv_acc[...] += conv_grad
            if conv_bias:
                conv_bias_acc[...] += functools.reduce(jnp.add, conv_bias)
            if out_bias:
                out_bias_acc[...] += functools.reduce(jnp.add, out_bias)
            if has(n - 1) and n * GROUP % (8 * across) == 0:
                copies.append(finish_losses(n * GROUP // (8 * across) - 1))
                copies[-1].start()
        return copies

    copies = run(tiles + 3)

    for k in range(turned_ref.shape[0]):
        turned_ref[k] = conv_acc[:, k * 128 : (k + 1) * 128]
    parts = []
    for tap in range(TAPS_X):
        kept = []
        for q in range(GROUP):
            lane = q * hidden % 128
            rows = pl.ds(q + 1 + tap, taps // WINDOW, stride=WINDOW)
            kept.append(turned_ref[q * hidden // 128, rows, :][:, lane : lane + hidden])
        parts.append(functools.reduce(jnp.add, kept))
    parts.append(jnp.sum(jnp.transpose(conv_bias_acc[...]), axis=0, keepdims=True))
    parts.append(jnp.sum(jnp.transpose(out_bias_acc[...]), axis=0, keepdims=True))
    spare = hidden - sum(part.shape[0] for part in parts)
    parts.append(jnp.zeros((spare, hidden), jnp.float32))
    grads_ref[...] = jnp.concatenate([jnp.concatenate(parts, axis=0), out_acc[...]], axis=1)
    for copy in copies:
        copy.wait()


def unpack(total_ref, conv_ref, conv_bias_ref, out_ref, out_bias_ref):
    used, hidden = conv_ref.shape
    conv_ref[...] = total_ref[:used, :hidden]
    conv_bias_ref[...] = total_ref[used : used + 1, :hidden]
    out_ref[...] = total_ref[:, hidden:]
    out_bias_ref[...] = total_ref[used + 1 : used + 2, :hidden]


AXES = ("sec", "sp", "dp")


def factors(size):
    stride = 1
    while stride < size:
        left = size // stride
        radix = next(p for p in range(2, left + 1) if left % p == 0)
        yield stride, radix
        stride *= radix


def moved(place, rounds, steps, sizes):
    for (axis, inner, radix), step in zip(rounds, steps):
        for size in sizes[axis + 1 :]:
            inner *= size
        digit = place // inner % radix
        place += ((digit + step) % radix - digit) * inner
    return place


def summed(value):
    sizes = [lax.axis_size(axis) for axis in AXES]
    total = sizes[0] * sizes[1] * sizes[2]
    rounds = [(axis, *f) for axis in (1, 0, 2) for f in factors(sizes[axis])]
    halvings = [r for r in rounds if r[2] == 2]
    groups = [halvings[:1]] + [halvings[i : i + 2] for i in range(1, len(halvings), 2)]
    groups += [[r] for r in rounds if r[2] != 2]

    def sent(rounds, steps):
        return lax.ppermute(
            value, AXES, [(i, moved(i, rounds, steps, sizes)) for i in range(total)]
        )

    for group in groups:
        if len(group) == 2:
            near, far, last = [sent(group, steps) for steps in ((1, 0), (0, 1), (1, 1))]
            value = (value + near) + (far + last)
        elif group[0][2] == 2:
            value = value + sent(group, (1,))
        else:
            axis, stride, radix = group[0]
            terms = [value] + [sent(group, (k,)) for k in range(1, radix)]
            mine = lax.axis_index(AXES[axis]) // stride % radix
            stacked = jnp.stack(terms + terms)[::-1]
            value = jnp.sum(lax.dynamic_slice_in_dim(stacked, radix - 1 - mine, radix), axis=0)
    return value


def three_terms(bias):
    terms = []
    for _ in range(3):
        term = bias.astype(jnp.bfloat16).astype(jnp.float32)
        terms.append(term)
        bias = bias - term
    return terms


def prepare(*refs):
    given, (banded_ref, out_t_ref, out_half_ref), turned_ref, held, sems = refs[:4], refs[4:7], *refs[7:]
    copies = [pltpu.make_async_copy(g, h, sems.at[k]) for k, (g, h) in enumerate(zip(given, held))]
    for copy in copies:
        copy.start()
    for copy in copies:
        copy.wait()
    conv_ref, conv_bias_ref, out_ref, out_bias_ref = held
    hidden, bins = out_ref.shape
    turned_ref[...] = jnp.zeros_like(turned_ref)
    conv = 0.5 * conv_ref[...].astype(jnp.float32)
    empty = jnp.zeros((2 * OFFSETS, hidden), jnp.float32)
    for q in range(GROUP):
        for tap in range(TAPS_X):
            part = conv[tap * 2 * OFFSETS : (tap + 1) * 2 * OFFSETS]
            pair = [part, empty] if q % 2 == 0 else [empty, part]
            rows = pl.ds(q + 1 + tap, 2 * OFFSETS, stride=WINDOW)
            turned_ref[q // 2, rows, :] += jnp.concatenate(pair, axis=1)
    center = (OFFSETS - 1) * WINDOW
    places = (center, center + WINDOW, center + WINDOW - 1)
    for row, term in zip(places, three_terms(0.5 * conv_bias_ref[...])):
        for k in range(GROUP // 2):
            turned_ref[k, row : row + 1, :] = jnp.concatenate([term, term], axis=1)
    for k in range(GROUP // 2):
        banded_ref[2 * k * hidden : 2 * (k + 1) * hidden, :] = jnp.transpose(turned_ref[k]).astype(
            jnp.bfloat16
        )
    out = out_ref[...].astype(jnp.float32)
    spare = jnp.zeros((out_t_ref.shape[1] - hidden - 3, bins), jnp.float32)
    extended = jnp.concatenate([out] + three_terms(out_bias_ref[...]) + [spare], axis=0)
    out_t_ref[...] = jnp.transpose(extended).astype(jnp.bfloat16)
    out_half_ref[...] = (0.5 * out).astype(jnp.bfloat16)


def prepared_weights(conv_weight, conv_bias, out_weight, out_bias):
    hidden, bins = out_weight.shape
    taps = 2 * OFFSETS * WINDOW
    vmem = pl.BlockSpec(memory_space=pltpu.VMEM)
    given = (conv_weight, conv_bias.reshape(1, hidden), out_weight, out_bias.reshape(1, bins))
    return pl.pallas_call(
        prepare,
        out_shape=(
            jax.ShapeDtypeStruct((GROUP * hidden, taps), jnp.bfloat16),
            jax.ShapeDtypeStruct((bins, hidden + 16), jnp.bfloat16),
            jax.ShapeDtypeStruct((hidden, bins), jnp.bfloat16),
        ),
        in_specs=[pl.BlockSpec(memory_space=pltpu.HBM)] * 4,
        out_specs=(vmem,) * 3,
        scratch_shapes=[
            pltpu.VMEM((GROUP // 2, taps, 2 * hidden), jnp.float32),
            [pltpu.VMEM(g.shape, g.dtype) for g in given],
            pltpu.SemaphoreType.DMA((4,)),
        ],
        compiler_params=pltpu.CompilerParams(vmem_limit_bytes=40 * 1024 * 1024),
        cost_estimate=pl.CostEstimate(flops=1000000, bytes_accessed=1000000, transcendentals=0),
        name="prepare",
    )(*given)


def shards(fraction, labels, conv_weight, conv_bias, out_weight, out_bias):
    sections = lax.axis_size("sec")
    brick = fraction[0]
    arrived = lax.all_to_all(brick, ("sec", "sp"), split_axis=0, concat_axis=1, tiled=True)
    width = arrived.shape[2]
    arrived = arrived.reshape(sections, -1, width)
    patch_labels = labels.reshape(labels.shape[2:])
    planes, plane = patch_labels.shape
    hidden, bins = out_weight.shape
    scale = 1.0 / (lax.axis_size("sec") * lax.axis_size("sp") * lax.axis_size("dp") * planes * plane)
    weights = prepared_weights(conv_weight, conv_bias, out_weight, out_bias)
    taps = weights[0].shape[1]
    vmem = pl.BlockSpec(memory_space=pltpu.VMEM)
    rows = GROUP * hidden
    loss, grads = pl.pallas_call(
        functools.partial(train_patch, scale),
        out_shape=(
            jax.ShapeDtypeStruct((planes, plane), jnp.float32),
            jax.ShapeDtypeStruct((hidden, hidden + bins), jnp.float32),
        ),
        in_specs=[vmem] * 5,
        out_specs=(pl.BlockSpec(memory_space=pl.ANY), vmem),
        scratch_shapes=[
            [pltpu.VMEM((taps, plane), jnp.bfloat16)] * (planes // GROUP),
            [[pltpu.VMEM((weights[1].shape[1], LANES), jnp.bfloat16)] * GROUP] * SLOTS,
            [[pltpu.VMEM((hidden, LANES), jnp.float32)] * GROUP] * SLOTS,
            [[pltpu.VMEM((bins, LANES), jnp.bfloat16)] * GROUP] * SLOTS,
            [[pltpu.VMEM((hidden, LANES), jnp.bfloat16)] * GROUP] * SLOTS,
            pltpu.VMEM((taps, rows), jnp.float32),
            pltpu.VMEM((hidden, bins), jnp.float32),
            pltpu.VMEM((hidden, 128), jnp.float32),
            pltpu.VMEM((bins, 128), jnp.float32),
            pltpu.VMEM((planes, plane), jnp.float32),
            pltpu.VMEM((planes, plane), jnp.float32),
            pltpu.VMEM((planes, plane), jnp.float32),
            pltpu.VMEM((rows // 128, taps, 128), jnp.float32),
            pltpu.SemaphoreType.DMA((planes // 8,)),
        ],
        compiler_params=pltpu.CompilerParams(vmem_limit_bytes=24 * 1024 * 1024),
        name="train_patch",
    )(arrived, patch_labels, *weights)
    shapes = (conv_weight.shape, (1, hidden), out_weight.shape, (1, bins))
    conv_grad, conv_bias_grad, out_grad, out_bias_grad = pl.pallas_call(
        unpack,
        out_shape=tuple(jax.ShapeDtypeStruct(shape, jnp.float32) for shape in shapes),
        in_specs=[vmem],
        out_specs=(vmem,) * 4,
        compiler_params=pltpu.CompilerParams(vmem_limit_bytes=8 * 1024 * 1024),
        name="unpack",
    )(summed(grads))
    return (
        loss.reshape(labels.shape),
        conv_grad,
        conv_bias_grad.reshape(conv_bias.shape),
        out_grad,
        out_bias_grad.reshape(out_bias.shape),
    )


def solution(mesh):
    placed = (P("dp", None, "sp", "sec"), P("dp", ("sec", "sp"), None, None), P(), P(), P(), P())
    return jax.shard_map(
        shards,
        mesh=mesh,
        in_specs=placed,
        out_specs=(P("dp", ("sec", "sp"), None, None), P(), P(), P(), P()),
        check_vma=False,
    )
```

```python
import functools

import jax
import jax.numpy as jnp
from jax import lax
from jax.experimental import pallas as pl
from jax.experimental.pallas import tpu as pltpu
from jax.sharding import PartitionSpec as P

PZ = 32
TAPS_X = 3
OFFSETS = 9
WINDOW = 8
GROUP = 4
LANES = 512
SLOTS = 4


def rolled(values, step, axis):
    size = values.shape[axis]
    return pltpu.roll(values, (-step) % size, axis)


def neighbour(values, step, axis, inside):
    return jnp.where(inside, rolled(values, step, axis), 0.0)


def window_rows(cells):
    planes, plane = cells.shape
    plane_x = lax.broadcasted_iota(jnp.int32, cells.shape, 0)
    lane = lax.broadcasted_iota(jnp.int32, cells.shape, 1)
    col_z = lane & (PZ - 1)
    has = {
        (0, -1): plane_x > 0,
        (0, 1): plane_x < planes - 1,
        (PZ, -1): lane >= PZ,
        (PZ, 1): lane < plane - PZ,
        (1, -1): col_z > 0,
        (1, 1): col_z < PZ - 1,
    }

    def box(values):
        for stride in (0, PZ, 1):
            axis = 1 if stride else 0
            step = stride or 1
            values = (
                neighbour(values, -step, axis, has[stride, -1])
                + values
                + neighbour(values, step, axis, has[stride, 1])
            )
        return values * (1.0 / 27.0)

    filt = box(cells)
    spread = box(cells * cells) - filt * filt
    channels = (filt, spread)
    place = plane_x & (WINDOW - 1)
    unused = (place == 0) | (place == WINDOW - 1)
    for side, (step, inside) in enumerate(((-2, plane_x >= 2), (2, plane_x < planes - 2))):
        pair = [jnp.where(unused, 1.0, neighbour(v, step, 0, inside)) for v in channels]
        for k in range(planes // WINDOW):
            rows = [v[k * WINDOW : (k + 1) * WINDOW] for v in pair]
            yield 2 * k + side, jnp.concatenate(rows, axis=0).astype(jnp.bfloat16)


def neighbour_rows(offset):
    return slice(offset * 2 * WINDOW, (offset + 1) * 2 * WINDOW)


def spread_window(window_ref, offset):
    both = window_ref[neighbour_rows(OFFSETS // 2), :]
    step_y, step_z = offset // 3 - 1, offset % 3 - 1
    lane = lax.broadcasted_iota(jnp.int32, both.shape, 1)
    row_y, col_z = lane + step_y * PZ, (lane & (PZ - 1)) + step_z
    inside = (row_y >= 0) & (row_y < both.shape[1]) & (col_z >= 0) & (col_z < PZ)
    values = rolled(both, step_y * PZ + step_z, 1)
    window_ref[neighbour_rows(offset), :] = jnp.where(inside, values, jnp.zeros((), both.dtype))


def contract_cells(left, right):
    return lax.dot_general(
        left, right, (((1,), (1,)), ((), ())), preferred_element_type=jnp.float32
    )


def fold_lanes(values):
    parts = [values[:, i : i + 128] for i in range(0, values.shape[1], 128)]
    return functools.reduce(jnp.add, parts)


def inverse(values):
    rough = pltpu.reciprocal(values, approx=True)
    return rough * (2.0 - values * rough)


def train_patch(
    scale, arrived_ref, labels_ref, conv_ref, out_t_ref, out_ref, loss_ref, grads_ref,
    windows, acts, slopes, residuals, hidden_low, conv_acc, out_acc, conv_bias_acc, out_bias_acc,
    sums, picked, losses, turned_ref, loss_sems,
):
    planes, plane = labels_ref.shape
    taps = conv_ref.shape[1]
    hidden, bins = out_ref.shape
    across = plane // LANES
    tiles = planes // GROUP * across
    cells = jnp.concatenate([arrived_ref[s] for s in range(arrived_ref.shape[0])], axis=1)
    for window, both in window_rows(cells):
        windows[window][neighbour_rows(OFFSETS // 2), :] = both
    beside = [offset for offset in range(OFFSETS) if offset != OFFSETS // 2]
    for offset in beside:
        spread_window(windows[0], offset)
    for ref in (conv_acc, out_acc, conv_bias_acc, out_bias_acc):
        ref[...] = jnp.zeros_like(ref)
    for refs in acts:
        for ref in refs:
            ref[hidden:, :] = jnp.ones((ref.shape[0] - hidden, LANES), jnp.bfloat16)
    bin_ids = lax.broadcasted_iota(jnp.int32, (bins, LANES), 0)

    def place(n):
        return n // across, pl.ds(n % across * LANES, LANES)

    def finish_losses(block):
        rows = pl.ds(block * 8, 8)
        losses[rows, :] = jnp.log(sums[rows, :]) - picked[rows, :]
        return pltpu.make_async_copy(losses.at[rows, :], loss_ref.at[rows, :], loss_sems.at[block])

    def dot(left, right):
        return jnp.dot(left, right, preferred_element_type=jnp.float32)

    halves = [None]

    def convolve(n, q):
        window, lanes = place(n)
        if q == 0:
            halves[0] = dot(conv_ref[...], windows[window][:, lanes])
        return halves[0][q * hidden : (q + 1) * hidden]

    def products(n, slot, q, back, soft, act):
        return (
            dot(out_ref[...], residuals[(slot - 2) % SLOTS][q][...]) if back else None,
            dot(out_t_ref[...], acts[(slot - 1) % SLOTS][q][...]) if soft else None,
            convolve(n, q) if act else None,
        )

    def project_grad(slot):
        slot = (slot - 3) % SLOTS
        return contract_cells(
            jnp.concatenate([ref[:hidden, :] for ref in acts[slot]], axis=1),
            jnp.concatenate([ref[...] for ref in residuals[slot]], axis=1),
        )

    def convolve_grad(n, slot):
        window, lanes = place(n - 3)
        return contract_cells(
            windows[window][:, lanes],
            jnp.concatenate([ref[...] for ref in hidden_low[(slot - 3) % SLOTS]], axis=0),
        )

    def unactivate(slot, q, back):
        slot = (slot - 2) % SLOTS
        hidden_grad = back * slopes[slot][q][...]
        hidden_low[slot][q][...] = hidden_grad.astype(jnp.bfloat16)
        return fold_lanes(hidden_grad)

    def soften(n, slot, q, logits):
        window, lanes = place(n - 1)
        row = pl.ds(window * GROUP + q, 1)
        exp_logits = jnp.exp(logits)
        partition = jnp.sum(exp_logits, axis=0, keepdims=True)
        is_label = bin_ids == labels_ref[row, lanes]
        sums[row, lanes] = partition
        picked[row, lanes] = jnp.sum(jnp.where(is_label, logits, 0.0), axis=0, keepdims=True)
        residual = exp_logits * (scale * inverse(partition)) - jnp.where(is_label, scale, 0.0)
        residuals[(slot - 1) % SLOTS][q][...] = residual.astype(jnp.bfloat16)
        return fold_lanes(residual)

    def activate(slot, q, half):
        tanh = jnp.tanh(half)
        upper = 1.0 + tanh
        act = half * upper
        acts[slot % SLOTS][q][:hidden, :] = act.astype(jnp.bfloat16)
        slopes[slot % SLOTS][q][...] = upper + act * (1.0 - tanh)

    def has(n):
        return 0 <= n < tiles

    def issue(n, q):
        return products(n, n, q, has(n - 2), has(n - 1), has(n))

    def run(count):
        ahead = issue(0, 0)
        copies = []
        share = pl.cdiv(len(beside), across * GROUP)
        for n in range(count):
            conv_bias, out_bias, out_grad, conv_grad = [], [], None, None
            for q in range(GROUP):
                back, logits, half = ahead
                if n // across + 1 < len(windows):
                    first = (n % across * GROUP + q) * share
                    for offset in beside[first : first + share]:
                        spread_window(windows[n // across + 1], offset)
                ahead = issue(n, q + 1) if q + 1 < GROUP else issue(n + 1, 0)
                if q == 0 and has(n - 3):
                    out_grad = project_grad(n)
                if q == 1 and has(n - 3):
                    conv_grad = convolve_grad(n, n)
                if back is not None:
                    conv_bias.append(unactivate(n, q, back))
                if logits is not None:
                    out_bias.append(soften(n, n, q, logits))
                if half is not None:
                    activate(n, q, half)
            if has(n - 3):
                out_acc[...] += out_grad
                conv_acc[...] += conv_grad
            if conv_bias:
                conv_bias_acc[...] += functools.reduce(jnp.add, conv_bias)
            if out_bias:
                out_bias_acc[...] += functools.reduce(jnp.add, out_bias)
            if has(n - 1) and n * GROUP % (8 * across) == 0:
                copies.append(finish_losses(n * GROUP // (8 * across) - 1))
                copies[-1].start()
        return copies

    copies = run(tiles + 3)

    for k in range(turned_ref.shape[0]):
        turned_ref[k] = conv_acc[:, k * 128 : (k + 1) * 128]
    parts = []
    for tap in range(TAPS_X):
        kept = []
        for q in range(GROUP):
            lane = q * hidden % 128
            rows = pl.ds(q + 1 + tap, taps // WINDOW, stride=WINDOW)
            kept.append(turned_ref[q * hidden // 128, rows, :][:, lane : lane + hidden])
        parts.append(functools.reduce(jnp.add, kept))
    parts.append(jnp.sum(jnp.transpose(conv_bias_acc[...]), axis=0, keepdims=True))
    parts.append(jnp.sum(jnp.transpose(out_bias_acc[...]), axis=0, keepdims=True))
    spare = hidden - sum(part.shape[0] for part in parts)
    parts.append(jnp.zeros((spare, hidden), jnp.float32))
    grads_ref[...] = jnp.concatenate([jnp.concatenate(parts, axis=0), out_acc[...]], axis=1)
    for copy in copies:
        copy.wait()


def unpack(mine_ref, back_ref, mask_ref, conv_ref, conv_bias_ref, out_ref, out_bias_ref):
    used, hidden = conv_ref.shape
    total = jnp.where(mask_ref[...] > 0.0, mine_ref[...], back_ref[...])
    conv_ref[...] = total[:used, :hidden]
    conv_bias_ref[...] = total[used : used + 1, :hidden]
    out_ref[...] = total[:, hidden:]
    out_bias_ref[...] = total[used + 1 : used + 2, :hidden]


AXES = ("sec", "sp", "dp")


def factors(size):
    stride = 1
    while stride < size:
        left = size // stride
        radix = next(p for p in range(2, left + 1) if left % p == 0)
        yield stride, radix
        stride *= radix


def moved(place, rounds, steps, sizes):
    for (axis, inner, radix), step in zip(rounds, steps):
        for size in sizes[axis + 1 :]:
            inner *= size
        digit = place // inner % radix
        place += ((digit + step) % radix - digit) * inner
    return place


def summed(value):
    sizes = [lax.axis_size(axis) for axis in AXES]
    total = sizes[0] * sizes[1] * sizes[2]
    rounds = [(axis, *f) for axis in (1, 0, 2) for f in factors(sizes[axis])]
    halvings = [r for r in rounds if r[2] == 2]
    cores, halvings = halvings[:1], halvings[1:]
    groups = [halvings[i : i + 2] for i in range(0, len(halvings), 2)]
    groups += [[r] for r in rounds if r[2] != 2]
    near_rounds = groups[0]

    def sent(rounds, steps):
        def target(i):
            if rounds not in (cores, near_rounds) and i // sizes[2] % 2 == 0:
                turn = (sum(steps) - steps[0]) % len(near_rounds) if len(steps) > 1 else steps[0] % len(near_rounds)
                return moved(i, [near_rounds[turn]], (1,), sizes)
            return moved(i, rounds, steps, sizes)

        return lax.ppermute(value, AXES, [(i, target(i)) for i in range(total)])

    value = value + sent(cores, (1,))
    for group in groups:
        if len(group) == 2:
            near, far, last = [sent(group, steps) for steps in ((1, 0), (0, 1), (1, 1))]
            value = (value + near) + (far + last)
        elif group[0][2] == 2:
            value = value + sent(group, (1,))
        else:
            axis, stride, radix = group[0]
            terms = [value] + [sent(group, (k,)) for k in range(1, radix)]
            mine = lax.axis_index(AXES[axis]) // stride % radix
            stacked = jnp.stack(terms + terms)[::-1]
            value = jnp.sum(lax.dynamic_slice_in_dim(stacked, radix - 1 - mine, radix), axis=0)
    return value, sent(cores, (1,))


def three_terms(bias):
    terms = []
    for _ in range(3):
        term = bias.astype(jnp.bfloat16).astype(jnp.float32)
        terms.append(term)
        bias = bias - term
    return terms


def prepare(*refs):
    given, (banded_ref, out_t_ref, out_half_ref), turned_ref, held, sems = refs[:4], refs[4:7], *refs[7:]
    copies = [pltpu.make_async_copy(g, h, sems.at[k]) for k, (g, h) in enumerate(zip(given, held))]
    for copy in copies:
        copy.start()
    for copy in copies:
        copy.wait()
    conv_ref, conv_bias_ref, out_ref, out_bias_ref = held
    hidden, bins = out_ref.shape
    turned_ref[...] = jnp.zeros_like(turned_ref)
    conv = 0.5 * conv_ref[...].astype(jnp.float32)
    empty = jnp.zeros((2 * OFFSETS, hidden), jnp.float32)
    for q in range(GROUP):
        for tap in range(TAPS_X):
            part = conv[tap * 2 * OFFSETS : (tap + 1) * 2 * OFFSETS]
            pair = [part, empty] if q % 2 == 0 else [empty, part]
            rows = pl.ds(q + 1 + tap, 2 * OFFSETS, stride=WINDOW)
            turned_ref[q // 2, rows, :] += jnp.concatenate(pair, axis=1)
    center = (OFFSETS - 1) * WINDOW
    places = (center, center + WINDOW, center + WINDOW - 1)
    for row, term in zip(places, three_terms(0.5 * conv_bias_ref[...])):
        for k in range(GROUP // 2):
            turned_ref[k, row : row + 1, :] = jnp.concatenate([term, term], axis=1)
    for k in range(GROUP // 2):
        banded_ref[2 * k * hidden : 2 * (k + 1) * hidden, :] = jnp.transpose(turned_ref[k]).astype(
            jnp.bfloat16
        )
    out = out_ref[...].astype(jnp.float32)
    spare = jnp.zeros((out_t_ref.shape[1] - hidden - 3, bins), jnp.float32)
    extended = jnp.concatenate([out] + three_terms(out_bias_ref[...]) + [spare], axis=0)
    out_t_ref[...] = jnp.transpose(extended).astype(jnp.bfloat16)
    out_half_ref[...] = (0.5 * out).astype(jnp.bfloat16)


def prepared_weights(conv_weight, conv_bias, out_weight, out_bias):
    hidden, bins = out_weight.shape
    taps = 2 * OFFSETS * WINDOW
    vmem = pl.BlockSpec(memory_space=pltpu.VMEM)
    given = (conv_weight, conv_bias.reshape(1, hidden), out_weight, out_bias.reshape(1, bins))
    return pl.pallas_call(
        prepare,
        out_shape=(
            jax.ShapeDtypeStruct((GROUP * hidden, taps), jnp.bfloat16),
            jax.ShapeDtypeStruct((bins, hidden + 16), jnp.bfloat16),
            jax.ShapeDtypeStruct((hidden, bins), jnp.bfloat16),
        ),
        in_specs=[pl.BlockSpec(memory_space=pltpu.HBM)] * 4,
        out_specs=(vmem,) * 3,
        scratch_shapes=[
            pltpu.VMEM((GROUP // 2, taps, 2 * hidden), jnp.float32),
            [pltpu.VMEM(g.shape, g.dtype) for g in given],
            pltpu.SemaphoreType.DMA((4,)),
        ],
        compiler_params=pltpu.CompilerParams(vmem_limit_bytes=40 * 1024 * 1024),
        cost_estimate=pl.CostEstimate(flops=1000000, bytes_accessed=1000000, transcendentals=0),
        name="prepare",
    )(*given)


def shards(fraction, labels, conv_weight, conv_bias, out_weight, out_bias):
    sections = lax.axis_size("sec")
    brick = fraction[0]
    arrived = lax.all_to_all(brick, ("sec", "sp"), split_axis=0, concat_axis=1, tiled=True)
    width = arrived.shape[2]
    arrived = arrived.reshape(sections, -1, width)
    patch_labels = labels.reshape(labels.shape[2:])
    planes, plane = patch_labels.shape
    hidden, bins = out_weight.shape
    scale = 1.0 / (lax.axis_size("sec") * lax.axis_size("sp") * lax.axis_size("dp") * planes * plane)
    weights = prepared_weights(conv_weight, conv_bias, out_weight, out_bias)
    taps = weights[0].shape[1]
    vmem = pl.BlockSpec(memory_space=pltpu.VMEM)
    core = (lax.axis_index("sp") & 1).astype(jnp.float32)
    mask = jnp.broadcast_to(core, (1, hidden + bins))
    arrived, mask = lax.optimization_barrier((arrived, mask))
    rows = GROUP * hidden
    loss, grads = pl.pallas_call(
        functools.partial(train_patch, scale),
        out_shape=(
            jax.ShapeDtypeStruct((planes, plane), jnp.float32),
            jax.ShapeDtypeStruct((hidden, hidden + bins), jnp.float32),
        ),
        in_specs=[vmem] * 5,
        out_specs=(pl.BlockSpec(memory_space=pl.ANY), vmem),
        scratch_shapes=[
            [pltpu.VMEM((taps, plane), jnp.bfloat16)] * (planes // GROUP),
            [[pltpu.VMEM((weights[1].shape[1], LANES), jnp.bfloat16)] * GROUP] * SLOTS,
            [[pltpu.VMEM((hidden, LANES), jnp.float32)] * GROUP] * SLOTS,
            [[pltpu.VMEM((bins, LANES), jnp.bfloat16)] * GROUP] * SLOTS,
            [[pltpu.VMEM((hidden, LANES), jnp.bfloat16)] * GROUP] * SLOTS,
            pltpu.VMEM((taps, rows), jnp.float32),
            pltpu.VMEM((hidden, bins), jnp.float32),
            pltpu.VMEM((hidden, 128), jnp.float32),
            pltpu.VMEM((bins, 128), jnp.float32),
            pltpu.VMEM((planes, plane), jnp.float32),
            pltpu.VMEM((planes, plane), jnp.float32),
            pltpu.VMEM((planes, plane), jnp.float32),
            pltpu.VMEM((rows // 128, taps, 128), jnp.float32),
            pltpu.SemaphoreType.DMA((planes // 8,)),
        ],
        compiler_params=pltpu.CompilerParams(vmem_limit_bytes=24 * 1024 * 1024),
        name="train_patch",
    )(arrived, patch_labels, *weights)
    shapes = (conv_weight.shape, (1, hidden), out_weight.shape, (1, bins))
    conv_grad, conv_bias_grad, out_grad, out_bias_grad = pl.pallas_call(
        unpack,
        out_shape=tuple(jax.ShapeDtypeStruct(shape, jnp.float32) for shape in shapes),
        in_specs=[vmem] * 3,
        out_specs=(vmem,) * 4,
        compiler_params=pltpu.CompilerParams(vmem_limit_bytes=8 * 1024 * 1024),
        name="unpack",
    )(*summed(grads), mask)
    return (
        loss.reshape(labels.shape),
        conv_grad,
        conv_bias_grad.reshape(conv_bias.shape),
        out_grad,
        out_bias_grad.reshape(out_bias.shape),
    )


def solution(mesh):
    placed = (P("dp", None, "sp", "sec"), P("dp", ("sec", "sp"), None, None), P(), P(), P(), P())
    return jax.shard_map(
        shards,
        mesh=mesh,
        in_specs=placed,
        out_specs=(P("dp", ("sec", "sp"), None, None), P(), P(), P(), P()),
        check_vma=False,
    )
```

```python
import functools

import jax
import jax.numpy as jnp
from jax import lax
from jax.experimental import pallas as pl
from jax.experimental.pallas import tpu as pltpu
from jax.sharding import PartitionSpec as P

PZ = 32
TAPS_X = 3
OFFSETS = 9
WINDOW = 8
GROUP = 4
LANES = 512
SLOTS = 4


def rolled(values, step, axis):
    size = values.shape[axis]
    return pltpu.roll(values, (-step) % size, axis)


def neighbour(values, step, axis, inside):
    return jnp.where(inside, rolled(values, step, axis), 0.0)


def window_rows(cells):
    planes, plane = cells.shape
    plane_x = lax.broadcasted_iota(jnp.int32, cells.shape, 0)
    lane = lax.broadcasted_iota(jnp.int32, cells.shape, 1)
    col_z = lane & (PZ - 1)
    has = {
        (0, -1): plane_x > 0,
        (0, 1): plane_x < planes - 1,
        (PZ, -1): lane >= PZ,
        (PZ, 1): lane < plane - PZ,
        (1, -1): col_z > 0,
        (1, 1): col_z < PZ - 1,
    }

    def box(values):
        for stride in (0, PZ, 1):
            axis = 1 if stride else 0
            step = stride or 1
            values = (
                neighbour(values, -step, axis, has[stride, -1])
                + values
                + neighbour(values, step, axis, has[stride, 1])
            )
        return values * (1.0 / 27.0)

    filt = box(cells)
    spread = box(cells * cells) - filt * filt
    channels = (filt, spread)
    place = plane_x & (WINDOW - 1)
    unused = (place == 0) | (place == WINDOW - 1)
    for side, (step, inside) in enumerate(((-2, plane_x >= 2), (2, plane_x < planes - 2))):
        pair = [jnp.where(unused, 1.0, neighbour(v, step, 0, inside)) for v in channels]
        for k in range(planes // WINDOW):
            rows = [v[k * WINDOW : (k + 1) * WINDOW] for v in pair]
            yield 2 * k + side, jnp.concatenate(rows, axis=0).astype(jnp.bfloat16)


def neighbour_rows(offset):
    return slice(offset * 2 * WINDOW, (offset + 1) * 2 * WINDOW)


def spread_window(window_ref, offset):
    both = window_ref[neighbour_rows(OFFSETS // 2), :]
    step_y, step_z = offset // 3 - 1, offset % 3 - 1
    lane = lax.broadcasted_iota(jnp.int32, both.shape, 1)
    row_y, col_z = lane + step_y * PZ, (lane & (PZ - 1)) + step_z
    inside = (row_y >= 0) & (row_y < both.shape[1]) & (col_z >= 0) & (col_z < PZ)
    values = rolled(both, step_y * PZ + step_z, 1)
    window_ref[neighbour_rows(offset), :] = jnp.where(inside, values, jnp.zeros((), both.dtype))


def contract_cells(left, right):
    return lax.dot_general(
        left, right, (((1,), (1,)), ((), ())), preferred_element_type=jnp.float32
    )


def fold_lanes(values):
    parts = [values[:, i : i + 128] for i in range(0, values.shape[1], 128)]
    return functools.reduce(jnp.add, parts)


def inverse(values):
    rough = pltpu.reciprocal(values, approx=True)
    return rough * (2.0 - values * rough)


def train_patch(
    scale, arrived_ref, labels_ref, conv_ref, out_t_ref, out_ref, loss_ref, grads_ref,
    windows, acts, slopes, residuals, hidden_low, conv_acc, out_acc, conv_bias_acc, out_bias_acc,
    sums, picked, losses, turned_ref, loss_sems,
):
    planes, plane = labels_ref.shape
    taps = conv_ref.shape[1]
    hidden, bins = out_ref.shape
    across = plane // LANES
    tiles = planes // GROUP * across
    cells = jnp.concatenate([arrived_ref[s] for s in range(arrived_ref.shape[0])], axis=1)
    for window, both in window_rows(cells):
        windows[window][neighbour_rows(OFFSETS // 2), :] = both
    beside = [offset for offset in range(OFFSETS) if offset != OFFSETS // 2]
    for offset in beside:
        spread_window(windows[0], offset)
    for ref in (conv_acc, out_acc, conv_bias_acc, out_bias_acc):
        ref[...] = jnp.zeros_like(ref)
    for refs in acts:
        for ref in refs:
            ref[hidden:, :] = jnp.ones((ref.shape[0] - hidden, LANES), jnp.bfloat16)
    bin_ids = lax.broadcasted_iota(jnp.int32, (bins, LANES), 0)

    def place(n):
        return n // across, pl.ds(n % across * LANES, LANES)

    def finish_losses(block):
        rows = pl.ds(block * 8, 8)
        losses[rows, :] = jnp.log(sums[rows, :]) - picked[rows, :]
        return pltpu.make_async_copy(losses.at[rows, :], loss_ref.at[rows, :], loss_sems.at[block])

    def dot(left, right):
        return jnp.dot(left, right, preferred_element_type=jnp.float32)

    halves = [None]

    def convolve(n, q):
        window, lanes = place(n)
        if q == 0:
            halves[0] = dot(conv_ref[...], windows[window][:, lanes])
        return halves[0][q * hidden : (q + 1) * hidden]

    def products(n, slot, q, back, soft, act):
        return (
            dot(out_ref[...], residuals[(slot - 2) % SLOTS][q][...]) if back else None,
            dot(out_t_ref[...], acts[(slot - 1) % SLOTS][q][...]) if soft else None,
            convolve(n, q) if act else None,
        )

    def project_grad(slot):
        slot = (slot - 3) % SLOTS
        return contract_cells(
            jnp.concatenate([ref[:hidden, :] for ref in acts[slot]], axis=1),
            jnp.concatenate([ref[...] for ref in residuals[slot]], axis=1),
        )

    def convolve_grad(n, slot):
        window, lanes = place(n - 3)
        return contract_cells(
            windows[window][:, lanes],
            jnp.concatenate([ref[...] for ref in hidden_low[(slot - 3) % SLOTS]], axis=0),
        )

    def unactivate(slot, q, back):
        slot = (slot - 2) % SLOTS
        hidden_grad = back * slopes[slot][q][...]
        hidden_low[slot][q][...] = hidden_grad.astype(jnp.bfloat16)
        return fold_lanes(hidden_grad)

    def soften(n, slot, q, logits):
        window, lanes = place(n - 1)
        row = pl.ds(window * GROUP + q, 1)
        exp_logits = jnp.exp(logits)
        partition = jnp.sum(exp_logits, axis=0, keepdims=True)
        is_label = bin_ids == labels_ref[row, lanes]
        sums[row, lanes] = partition
        picked[row, lanes] = jnp.sum(jnp.where(is_label, logits, 0.0), axis=0, keepdims=True)
        residual = exp_logits * (scale * inverse(partition)) - jnp.where(is_label, scale, 0.0)
        residuals[(slot - 1) % SLOTS][q][...] = residual.astype(jnp.bfloat16)
        return fold_lanes(residual)

    def activate(slot, q, half):
        tanh = jnp.tanh(half)
        upper = 1.0 + tanh
        act = half * upper
        acts[slot % SLOTS][q][:hidden, :] = act.astype(jnp.bfloat16)
        slopes[slot % SLOTS][q][...] = upper + act * (1.0 - tanh)

    def has(n):
        return 0 <= n < tiles

    def issue(n, q):
        return products(n, n, q, has(n - 2), has(n - 1), has(n))

    def run(count):
        ahead = issue(0, 0)
        copies = []
        share = pl.cdiv(len(beside), across * GROUP)
        for n in range(count):
            conv_bias, out_bias, out_grad, conv_grad = [], [], None, None
            for q in range(GROUP):
                back, logits, half = ahead
                if n // across + 1 < len(windows):
                    first = (n % across * GROUP + q) * share
                    for offset in beside[first : first + share]:
                        spread_window(windows[n // across + 1], offset)
                ahead = issue(n, q + 1) if q + 1 < GROUP else issue(n + 1, 0)
                if q == 0 and has(n - 3):
                    out_grad = project_grad(n)
                if q == 1 and has(n - 3):
                    conv_grad = convolve_grad(n, n)
                if back is not None:
                    conv_bias.append(unactivate(n, q, back))
                if logits is not None:
                    out_bias.append(soften(n, n, q, logits))
                if half is not None:
                    activate(n, q, half)
            if has(n - 3):
                out_acc[...] += out_grad
                conv_acc[...] += conv_grad
            if conv_bias:
                conv_bias_acc[...] += functools.reduce(jnp.add, conv_bias)
            if out_bias:
                out_bias_acc[...] += functools.reduce(jnp.add, out_bias)
            if has(n - 1) and n * GROUP % (8 * across) == 0:
                copies.append(finish_losses(n * GROUP // (8 * across) - 1))
                copies[-1].start()
        return copies

    copies = run(tiles + 3)

    for k in range(turned_ref.shape[0]):
        turned_ref[k] = conv_acc[:, k * 128 : (k + 1) * 128]
    parts = []
    for tap in range(TAPS_X):
        kept = []
        for q in range(GROUP):
            lane = q * hidden % 128
            rows = pl.ds(q + 1 + tap, taps // WINDOW, stride=WINDOW)
            kept.append(turned_ref[q * hidden // 128, rows, :][:, lane : lane + hidden])
        parts.append(functools.reduce(jnp.add, kept))
    parts.append(jnp.sum(jnp.transpose(conv_bias_acc[...]), axis=0, keepdims=True))
    parts.append(jnp.sum(jnp.transpose(out_bias_acc[...]), axis=0, keepdims=True))
    spare = hidden - sum(part.shape[0] for part in parts)
    parts.append(jnp.zeros((spare, hidden), jnp.float32))
    grads_ref[...] = jnp.concatenate([jnp.concatenate(parts, axis=0), out_acc[...]], axis=1)
    for copy in copies:
        copy.wait()


def unpack(mine_ref, other_ref, conv_ref, conv_bias_ref, out_ref, out_bias_ref):
    used, hidden = conv_ref.shape
    total = mine_ref[...] + other_ref[...]
    conv_ref[...] = total[:used, :hidden]
    conv_bias_ref[...] = total[used : used + 1, :hidden]
    out_ref[...] = total[:, hidden:]
    out_bias_ref[...] = total[used + 1 : used + 2, :hidden]


AXES = ("sec", "sp", "dp")


def factors(size):
    stride = 1
    while stride < size:
        left = size // stride
        radix = next(p for p in range(2, left + 1) if left % p == 0)
        yield stride, radix
        stride *= radix


def moved(place, rounds, steps, sizes):
    for (axis, inner, radix), step in zip(rounds, steps):
        for size in sizes[axis + 1 :]:
            inner *= size
        digit = place // inner % radix
        place += ((digit + step) % radix - digit) * inner
    return place


def summed(value, mask):
    sizes = [lax.axis_size(axis) for axis in AXES]
    total = sizes[0] * sizes[1] * sizes[2]
    rounds = [(axis, *f) for axis in (1, 0, 2) for f in factors(sizes[axis])]
    halvings = [r for r in rounds if r[2] == 2]
    cores, halvings = halvings[:1], halvings[1:]
    near = halvings[:1]
    groups = [[r] for r in rounds if r[2] != 2] + [halvings[-1:]] * (len(halvings) % 2)
    groups += [halvings[i : i + 2] for i in range(0, len(halvings) - 1, 2)]

    def sent(value, even, odd):
        return lax.ppermute(
            value,
            AXES,
            [(i, moved(i, *(odd if i // sizes[2] % 2 else even), sizes)) for i in range(total)],
        )

    def alike(value, rounds, steps):
        return sent(value, (rounds, steps), (rounds, steps))

    parts = value, alike(value, cores, (1,))
    for group in groups:
        value = parts[0] + parts[1]
        if len(group) == 2:
            first = sent(value, (group, (1, 0)), (group, (0, 1)))
            second = sent(value, (near, (1,)), (group, (1, 1)))
            part = first + jnp.where(mask > 0.0, second, value)
            parts = part, alike(part, cores, (1,))
        elif group[0][2] == 2:
            parts = value, alike(value, group, (1,))
        else:
            axis, stride, radix = group[0]
            terms = [value] + [alike(value, group, (k,)) for k in range(1, radix)]
            mine = lax.axis_index(AXES[axis]) // stride % radix
            stacked = jnp.stack(terms + terms)[::-1]
            ordered = lax.dynamic_slice_in_dim(stacked, radix - 1 - mine, radix)
            parts = ordered[0], jnp.sum(ordered[1:], axis=0)
    return parts


def three_terms(bias):
    terms = []
    for _ in range(3):
        term = bias.astype(jnp.bfloat16).astype(jnp.float32)
        terms.append(term)
        bias = bias - term
    return terms


def prepare(*refs):
    given, (banded_ref, out_t_ref, out_half_ref), turned_ref, held, sems = refs[:4], refs[4:7], *refs[7:]
    copies = [pltpu.make_async_copy(g, h, sems.at[k]) for k, (g, h) in enumerate(zip(given, held))]
    for copy in copies:
        copy.start()
    for copy in copies:
        copy.wait()
    conv_ref, conv_bias_ref, out_ref, out_bias_ref = held
    hidden, bins = out_ref.shape
    turned_ref[...] = jnp.zeros_like(turned_ref)
    conv = 0.5 * conv_ref[...].astype(jnp.float32)
    empty = jnp.zeros((2 * OFFSETS, hidden), jnp.float32)
    for q in range(GROUP):
        for tap in range(TAPS_X):
            part = conv[tap * 2 * OFFSETS : (tap + 1) * 2 * OFFSETS]
            pair = [part, empty] if q % 2 == 0 else [empty, part]
            rows = pl.ds(q + 1 + tap, 2 * OFFSETS, stride=WINDOW)
            turned_ref[q // 2, rows, :] += jnp.concatenate(pair, axis=1)
    center = (OFFSETS - 1) * WINDOW
    places = (center, center + WINDOW, center + WINDOW - 1)
    for row, term in zip(places, three_terms(0.5 * conv_bias_ref[...])):
        for k in range(GROUP // 2):
            turned_ref[k, row : row + 1, :] = jnp.concatenate([term, term], axis=1)
    for k in range(GROUP // 2):
        banded_ref[2 * k * hidden : 2 * (k + 1) * hidden, :] = jnp.transpose(turned_ref[k]).astype(
            jnp.bfloat16
        )
    out = out_ref[...].astype(jnp.float32)
    spare = jnp.zeros((out_t_ref.shape[1] - hidden - 3, bins), jnp.float32)
    extended = jnp.concatenate([out] + three_terms(out_bias_ref[...]) + [spare], axis=0)
    out_t_ref[...] = jnp.transpose(extended).astype(jnp.bfloat16)
    out_half_ref[...] = (0.5 * out).astype(jnp.bfloat16)


def prepared_weights(conv_weight, conv_bias, out_weight, out_bias):
    hidden, bins = out_weight.shape
    taps = 2 * OFFSETS * WINDOW
    vmem = pl.BlockSpec(memory_space=pltpu.VMEM)
    given = (conv_weight, conv_bias.reshape(1, hidden), out_weight, out_bias.reshape(1, bins))
    return pl.pallas_call(
        prepare,
        out_shape=(
            jax.ShapeDtypeStruct((GROUP * hidden, taps), jnp.bfloat16),
            jax.ShapeDtypeStruct((bins, hidden + 16), jnp.bfloat16),
            jax.ShapeDtypeStruct((hidden, bins), jnp.bfloat16),
        ),
        in_specs=[pl.BlockSpec(memory_space=pltpu.HBM)] * 4,
        out_specs=(vmem,) * 3,
        scratch_shapes=[
            pltpu.VMEM((GROUP // 2, taps, 2 * hidden), jnp.float32),
            [pltpu.VMEM(g.shape, g.dtype) for g in given],
            pltpu.SemaphoreType.DMA((4,)),
        ],
        compiler_params=pltpu.CompilerParams(vmem_limit_bytes=40 * 1024 * 1024),
        cost_estimate=pl.CostEstimate(flops=1000000, bytes_accessed=1000000, transcendentals=0),
        name="prepare",
    )(*given)


def shards(fraction, labels, conv_weight, conv_bias, out_weight, out_bias):
    sections = lax.axis_size("sec")
    brick = fraction[0]
    arrived = lax.all_to_all(brick, ("sec", "sp"), split_axis=0, concat_axis=1, tiled=True)
    width = arrived.shape[2]
    arrived = arrived.reshape(sections, -1, width)
    patch_labels = labels.reshape(labels.shape[2:])
    planes, plane = patch_labels.shape
    hidden, bins = out_weight.shape
    scale = 1.0 / (lax.axis_size("sec") * lax.axis_size("sp") * lax.axis_size("dp") * planes * plane)
    weights = prepared_weights(conv_weight, conv_bias, out_weight, out_bias)
    taps = weights[0].shape[1]
    vmem = pl.BlockSpec(memory_space=pltpu.VMEM)
    core = (lax.axis_index("sp") & 1).astype(jnp.float32)
    mask = jnp.broadcast_to(core, (hidden, hidden + bins))
    arrived, mask = lax.optimization_barrier((arrived, mask))
    rows = GROUP * hidden
    loss, grads = pl.pallas_call(
        functools.partial(train_patch, scale),
        out_shape=(
            jax.ShapeDtypeStruct((planes, plane), jnp.float32),
            jax.ShapeDtypeStruct((hidden, hidden + bins), jnp.float32),
        ),
        in_specs=[vmem] * 5,
        out_specs=(pl.BlockSpec(memory_space=pl.ANY), vmem),
        scratch_shapes=[
            [pltpu.VMEM((taps, plane), jnp.bfloat16)] * (planes // GROUP),
            [[pltpu.VMEM((weights[1].shape[1], LANES), jnp.bfloat16)] * GROUP] * SLOTS,
            [[pltpu.VMEM((hidden, LANES), jnp.float32)] * GROUP] * SLOTS,
            [[pltpu.VMEM((bins, LANES), jnp.bfloat16)] * GROUP] * SLOTS,
            [[pltpu.VMEM((hidden, LANES), jnp.bfloat16)] * GROUP] * SLOTS,
            pltpu.VMEM((taps, rows), jnp.float32),
            pltpu.VMEM((hidden, bins), jnp.float32),
            pltpu.VMEM((hidden, 128), jnp.float32),
            pltpu.VMEM((bins, 128), jnp.float32),
            pltpu.VMEM((planes, plane), jnp.float32),
            pltpu.VMEM((planes, plane), jnp.float32),
            pltpu.VMEM((planes, plane), jnp.float32),
            pltpu.VMEM((rows // 128, taps, 128), jnp.float32),
            pltpu.SemaphoreType.DMA((planes // 8,)),
        ],
        compiler_params=pltpu.CompilerParams(vmem_limit_bytes=24 * 1024 * 1024),
        name="train_patch",
    )(arrived, patch_labels, *weights)
    shapes = (conv_weight.shape, (1, hidden), out_weight.shape, (1, bins))
    conv_grad, conv_bias_grad, out_grad, out_bias_grad = pl.pallas_call(
        unpack,
        out_shape=tuple(jax.ShapeDtypeStruct(shape, jnp.float32) for shape in shapes),
        in_specs=[vmem] * 2,
        out_specs=(vmem,) * 4,
        compiler_params=pltpu.CompilerParams(vmem_limit_bytes=8 * 1024 * 1024),
        name="unpack",
    )(*summed(grads, mask))
    return (
        loss.reshape(labels.shape),
        conv_grad,
        conv_bias_grad.reshape(conv_bias.shape),
        out_grad,
        out_bias_grad.reshape(out_bias.shape),
    )


def solution(mesh):
    placed = (P("dp", None, "sp", "sec"), P("dp", ("sec", "sp"), None, None), P(), P(), P(), P())
    return jax.shard_map(
        shards,
        mesh=mesh,
        in_specs=placed,
        out_specs=(P("dp", ("sec", "sp"), None, None), P(), P(), P(), P()),
        check_vma=False,
    )
```

```python
import functools

import jax
import jax.numpy as jnp
from jax import lax
from jax.experimental import pallas as pl
from jax.experimental.pallas import tpu as pltpu
from jax.sharding import PartitionSpec as P

PZ = 32
TAPS_X = 3
OFFSETS = 9
WINDOW = 8
GROUP = 4
LANES = 512
SLOTS = 4


def rolled(values, step, axis):
    size = values.shape[axis]
    return pltpu.roll(values, (-step) % size, axis)


def neighbour(values, step, axis, inside):
    return jnp.where(inside, rolled(values, step, axis), 0.0)


def window_rows(cells):
    planes, plane = cells.shape
    plane_x = lax.broadcasted_iota(jnp.int32, cells.shape, 0)
    lane = lax.broadcasted_iota(jnp.int32, cells.shape, 1)
    col_z = lane & (PZ - 1)
    has = {
        (0, -1): plane_x > 0,
        (0, 1): plane_x < planes - 1,
        (PZ, -1): lane >= PZ,
        (PZ, 1): lane < plane - PZ,
        (1, -1): col_z > 0,
        (1, 1): col_z < PZ - 1,
    }

    def box(values):
        for stride in (0, PZ, 1):
            axis = 1 if stride else 0
            step = stride or 1
            values = (
                neighbour(values, -step, axis, has[stride, -1])
                + values
                + neighbour(values, step, axis, has[stride, 1])
            )
        return values * (1.0 / 27.0)

    filt = box(cells)
    spread = box(cells * cells) - filt * filt
    channels = (filt, spread)
    place = plane_x & (WINDOW - 1)
    unused = (place == 0) | (place == WINDOW - 1)
    for side, (step, inside) in enumerate(((-2, plane_x >= 2), (2, plane_x < planes - 2))):
        pair = [jnp.where(unused, 1.0, neighbour(v, step, 0, inside)) for v in channels]
        for k in range(planes // WINDOW):
            rows = [v[k * WINDOW : (k + 1) * WINDOW] for v in pair]
            yield 2 * k + side, jnp.concatenate(rows, axis=0).astype(jnp.bfloat16)


def neighbour_rows(offset):
    return slice(offset * 2 * WINDOW, (offset + 1) * 2 * WINDOW)


def spread_window(window_ref, offset):
    both = window_ref[neighbour_rows(OFFSETS // 2), :]
    step_y, step_z = offset // 3 - 1, offset % 3 - 1
    lane = lax.broadcasted_iota(jnp.int32, both.shape, 1)
    row_y, col_z = lane + step_y * PZ, (lane & (PZ - 1)) + step_z
    inside = (row_y >= 0) & (row_y < both.shape[1]) & (col_z >= 0) & (col_z < PZ)
    values = rolled(both, step_y * PZ + step_z, 1)
    window_ref[neighbour_rows(offset), :] = jnp.where(inside, values, jnp.zeros((), both.dtype))


def contract_cells(left, right):
    return lax.dot_general(
        left, right, (((1,), (1,)), ((), ())), preferred_element_type=jnp.float32
    )


def fold_lanes(values):
    parts = [values[:, i : i + 128] for i in range(0, values.shape[1], 128)]
    return functools.reduce(jnp.add, parts)


def inverse(values):
    rough = pltpu.reciprocal(values, approx=True)
    return rough * (2.0 - values * rough)


def train_patch(
    scale, arrived_ref, labels_ref, conv_ref, out_t_ref, out_ref, loss_ref, grads_ref,
    windows, acts, slopes, residuals, hidden_low, conv_acc, out_acc, conv_bias_acc, out_bias_acc,
    sums, picked, losses, turned_ref, loss_sems,
):
    planes, plane = labels_ref.shape
    taps = conv_ref.shape[1]
    hidden, bins = out_ref.shape
    across = plane // LANES
    tiles = planes // GROUP * across
    cells = jnp.concatenate([arrived_ref[s] for s in range(arrived_ref.shape[0])], axis=1)
    for window, both in window_rows(cells):
        windows[window][neighbour_rows(OFFSETS // 2), :] = both
    beside = [offset for offset in range(OFFSETS) if offset != OFFSETS // 2]
    for offset in beside:
        spread_window(windows[0], offset)
    for ref in (conv_acc, out_acc, conv_bias_acc, out_bias_acc):
        ref[...] = jnp.zeros_like(ref)
    for refs in acts:
        for ref in refs:
            ref[hidden:, :] = jnp.ones((ref.shape[0] - hidden, LANES), jnp.bfloat16)
    bin_ids = lax.broadcasted_iota(jnp.int32, (bins, LANES), 0).astype(jnp.float32)

    def place(n):
        return n // across, pl.ds(n % across * LANES, LANES)

    def finish_losses(block):
        rows = pl.ds(block * 8, 8)
        losses[rows, :] = jnp.log(sums[rows, :]) - picked[rows, :]
        return pltpu.make_async_copy(losses.at[rows, :], loss_ref.at[rows, :], loss_sems.at[block])

    def dot(left, right):
        return jnp.dot(left, right, preferred_element_type=jnp.float32)

    halves = [None]

    def convolve(n, q):
        window, lanes = place(n)
        if q == 0:
            halves[0] = dot(conv_ref[...], windows[window][:, lanes])
        return halves[0][q * hidden : (q + 1) * hidden]

    def products(n, slot, q, back, soft, act):
        return (
            dot(out_ref[...], residuals[(slot - 2) % SLOTS][q][...]) if back else None,
            dot(out_t_ref[...], acts[(slot - 1) % SLOTS][q][...]) if soft else None,
            convolve(n, q) if act else None,
        )

    def project_grad(slot):
        slot = (slot - 3) % SLOTS
        return contract_cells(
            jnp.concatenate([ref[:hidden, :] for ref in acts[slot]], axis=1),
            jnp.concatenate([ref[...] for ref in residuals[slot]], axis=1),
        )

    def convolve_grad(n, slot):
        window, lanes = place(n - 3)
        return contract_cells(
            windows[window][:, lanes],
            jnp.concatenate([ref[...] for ref in hidden_low[(slot - 3) % SLOTS]], axis=0),
        )

    def unactivate(slot, q, back):
        slot = (slot - 2) % SLOTS
        hidden_grad = back * slopes[slot][q][...]
        hidden_low[slot][q][...] = hidden_grad.astype(jnp.bfloat16)
        return fold_lanes(hidden_grad)

    def soften(n, slot, q, logits):
        window, lanes = place(n - 1)
        row = pl.ds(window * GROUP + q, 1)
        exp_logits = jnp.exp(logits)
        partition = jnp.sum(exp_logits, axis=0, keepdims=True)
        is_label = bin_ids == labels_ref[row, lanes]
        sums[row, lanes] = partition
        chosen = jnp.where(is_label, scale, 0.0)
        picked[row, lanes] = jnp.sum(chosen * logits, axis=0, keepdims=True) * (1.0 / scale)
        residual = exp_logits * (scale * inverse(partition)) - chosen
        residuals[(slot - 1) % SLOTS][q][...] = residual.astype(jnp.bfloat16)
        return fold_lanes(residual)

    def activate(slot, q, half):
        tanh = jnp.tanh(half)
        upper = 1.0 + tanh
        act = half * upper
        acts[slot % SLOTS][q][:hidden, :] = act.astype(jnp.bfloat16)
        slopes[slot % SLOTS][q][...] = upper + act * (1.0 - tanh)

    def has(n):
        return 0 <= n < tiles

    def issue(n, q):
        return products(n, n, q, has(n - 2), has(n - 1), has(n))

    def run(count):
        ahead = issue(0, 0)
        copies = []
        share = pl.cdiv(len(beside), across * GROUP)
        for n in range(count):
            conv_bias, out_bias, out_grad, conv_grad = [], [], None, None
            for q in range(GROUP):
                back, logits, half = ahead
                if n // across + 1 < len(windows):
                    first = (n % across * GROUP + q) * share
                    for offset in beside[first : first + share]:
                        spread_window(windows[n // across + 1], offset)
                ahead = issue(n, q + 1) if q + 1 < GROUP else issue(n + 1, 0)
                if q == 0 and has(n - 3):
                    out_grad = project_grad(n)
                if q == 1 and has(n - 3):
                    conv_grad = convolve_grad(n, n)
                if back is not None:
                    conv_bias.append(unactivate(n, q, back))
                if logits is not None:
                    out_bias.append(soften(n, n, q, logits))
                if half is not None:
                    activate(n, q, half)
            if has(n - 3):
                out_acc[...] += out_grad
                conv_acc[...] += conv_grad
            if conv_bias:
                conv_bias_acc[...] += functools.reduce(jnp.add, conv_bias)
            if out_bias:
                out_bias_acc[...] += functools.reduce(jnp.add, out_bias)
            if has(n - 1) and n * GROUP % (8 * across) == 0:
                copies.append(finish_losses(n * GROUP // (8 * across) - 1))
                copies[-1].start()
        return copies

    copies = run(tiles + 3)

    for k in range(turned_ref.shape[0]):
        turned_ref[k] = conv_acc[:, k * 128 : (k + 1) * 128]
    parts = []
    for tap in range(TAPS_X):
        kept = []
        for q in range(GROUP):
            lane = q * hidden % 128
            rows = pl.ds(q + 1 + tap, taps // WINDOW, stride=WINDOW)
            kept.append(turned_ref[q * hidden // 128, rows, :][:, lane : lane + hidden])
        parts.append(functools.reduce(jnp.add, kept))
    parts.append(jnp.sum(jnp.transpose(conv_bias_acc[...]), axis=0, keepdims=True))
    parts.append(jnp.sum(jnp.transpose(out_bias_acc[...]), axis=0, keepdims=True))
    spare = hidden - sum(part.shape[0] for part in parts)
    parts.append(jnp.zeros((spare, hidden), jnp.float32))
    grads_ref[...] = jnp.concatenate([jnp.concatenate(parts, axis=0), out_acc[...]], axis=1)
    for copy in copies:
        copy.wait()


def unpack(mine_ref, back_ref, mask_ref, conv_ref, conv_bias_ref, out_ref, out_bias_ref):
    used, hidden = conv_ref.shape
    total = jnp.where(mask_ref[...] > 0.0, mine_ref[...], back_ref[...])
    conv_ref[...] = total[:used, :hidden]
    conv_bias_ref[...] = total[used : used + 1, :hidden]
    out_ref[...] = total[:, hidden:]
    out_bias_ref[...] = total[used + 1 : used + 2, :hidden]


AXES = ("sec", "sp", "dp")


def factors(size):
    stride = 1
    while stride < size:
        left = size // stride
        radix = next(p for p in range(2, left + 1) if left % p == 0)
        yield stride, radix
        stride *= radix


def moved(place, rounds, steps, sizes):
    for (axis, inner, radix), step in zip(rounds, steps):
        for size in sizes[axis + 1 :]:
            inner *= size
        digit = place // inner % radix
        place += ((digit + step) % radix - digit) * inner
    return place


def summed(value):
    sizes = [lax.axis_size(axis) for axis in AXES]
    total = sizes[0] * sizes[1] * sizes[2]
    rounds = [(axis, *f) for axis in (1, 0, 2) for f in factors(sizes[axis])]
    halvings = [r for r in rounds if r[2] == 2]
    cores, halvings = halvings[:1], halvings[1:]
    groups = [halvings[i : i + 2] for i in range(0, len(halvings), 2)]
    groups += [[r] for r in rounds if r[2] != 2]
    near_rounds = groups[0]

    def sent(rounds, steps):
        def target(i):
            if rounds not in (cores, near_rounds) and i // sizes[2] % 2 == 0:
                turn = (sum(steps) - steps[0]) % len(near_rounds) if len(steps) > 1 else steps[0] % len(near_rounds)
                return moved(i, [near_rounds[turn]], (1,), sizes)
            return moved(i, rounds, steps, sizes)

        return lax.ppermute(value, AXES, [(i, target(i)) for i in range(total)])

    value = value + sent(cores, (1,))
    for group in groups:
        if len(group) == 2:
            last, far, near = [sent(group, steps) for steps in ((1, 1), (0, 1), (1, 0))]
            value = (value + near) + (far + last)
        elif group[0][2] == 2:
            value = value + sent(group, (1,))
        else:
            axis, stride, radix = group[0]
            terms = [value] + [sent(group, (k,)) for k in range(1, radix)]
            mine = lax.axis_index(AXES[axis]) // stride % radix
            stacked = jnp.stack(terms + terms)[::-1]
            value = jnp.sum(lax.dynamic_slice_in_dim(stacked, radix - 1 - mine, radix), axis=0)
    return value, sent(cores, (1,))


def three_terms(bias):
    terms = []
    for _ in range(3):
        term = bias.astype(jnp.bfloat16).astype(jnp.float32)
        terms.append(term)
        bias = bias - term
    return terms


def prepare(*refs):
    given, (banded_ref, out_t_ref, out_half_ref), turned_ref, held, sems = refs[:4], refs[4:7], *refs[7:]
    copies = [pltpu.make_async_copy(g, h, sems.at[k]) for k, (g, h) in enumerate(zip(given, held))]
    for copy in copies:
        copy.start()
    for copy in copies:
        copy.wait()
    conv_ref, conv_bias_ref, out_ref, out_bias_ref = held
    hidden, bins = out_ref.shape
    turned_ref[...] = jnp.zeros_like(turned_ref)
    conv = 0.5 * conv_ref[...].astype(jnp.float32)
    empty = jnp.zeros((2 * OFFSETS, hidden), jnp.float32)
    for q in range(GROUP):
        for tap in range(TAPS_X):
            part = conv[tap * 2 * OFFSETS : (tap + 1) * 2 * OFFSETS]
            pair = [part, empty] if q % 2 == 0 else [empty, part]
            rows = pl.ds(q + 1 + tap, 2 * OFFSETS, stride=WINDOW)
            turned_ref[q // 2, rows, :] += jnp.concatenate(pair, axis=1)
    center = (OFFSETS - 1) * WINDOW
    places = (center, center + WINDOW, center + WINDOW - 1)
    for row, term in zip(places, three_terms(0.5 * conv_bias_ref[...])):
        for k in range(GROUP // 2):
            turned_ref[k, row : row + 1, :] = jnp.concatenate([term, term], axis=1)
    for k in range(GROUP // 2):
        banded_ref[2 * k * hidden : 2 * (k + 1) * hidden, :] = jnp.transpose(turned_ref[k]).astype(
            jnp.bfloat16
        )
    out = out_ref[...].astype(jnp.float32)
    spare = jnp.zeros((out_t_ref.shape[1] - hidden - 3, bins), jnp.float32)
    extended = jnp.concatenate([out] + three_terms(out_bias_ref[...]) + [spare], axis=0)
    out_t_ref[...] = jnp.transpose(extended).astype(jnp.bfloat16)
    out_half_ref[...] = (0.5 * out).astype(jnp.bfloat16)


def prepared_weights(conv_weight, conv_bias, out_weight, out_bias):
    hidden, bins = out_weight.shape
    taps = 2 * OFFSETS * WINDOW
    vmem = pl.BlockSpec(memory_space=pltpu.VMEM)
    given = (conv_weight, conv_bias.reshape(1, hidden), out_weight, out_bias.reshape(1, bins))
    return pl.pallas_call(
        prepare,
        out_shape=(
            jax.ShapeDtypeStruct((GROUP * hidden, taps), jnp.bfloat16),
            jax.ShapeDtypeStruct((bins, hidden + 16), jnp.bfloat16),
            jax.ShapeDtypeStruct((hidden, bins), jnp.bfloat16),
        ),
        in_specs=[pl.BlockSpec(memory_space=pltpu.HBM)] * 4,
        out_specs=(vmem,) * 3,
        scratch_shapes=[
            pltpu.VMEM((GROUP // 2, taps, 2 * hidden), jnp.float32),
            [pltpu.VMEM(g.shape, g.dtype) for g in given],
            pltpu.SemaphoreType.DMA((4,)),
        ],
        compiler_params=pltpu.CompilerParams(vmem_limit_bytes=40 * 1024 * 1024),
        cost_estimate=pl.CostEstimate(flops=1000000, bytes_accessed=1000000, transcendentals=0),
        name="prepare",
    )(*given)


def shards(fraction, labels, conv_weight, conv_bias, out_weight, out_bias):
    sections = lax.axis_size("sec")
    brick = fraction[0]
    arrived = lax.all_to_all(brick, ("sec", "sp"), split_axis=0, concat_axis=1, tiled=True)
    width = arrived.shape[2]
    arrived = arrived.reshape(sections, -1, width)
    patch_labels = labels.reshape(labels.shape[2:]).astype(jnp.float32)
    planes, plane = patch_labels.shape
    hidden, bins = out_weight.shape
    scale = 1.0 / (lax.axis_size("sec") * lax.axis_size("sp") * lax.axis_size("dp") * planes * plane)
    weights = prepared_weights(conv_weight, conv_bias, out_weight, out_bias)
    taps = weights[0].shape[1]
    vmem = pl.BlockSpec(memory_space=pltpu.VMEM)
    core = (lax.axis_index("sp") & 1).astype(jnp.float32)
    mask = jnp.broadcast_to(core, (1, hidden + bins))
    arrived, mask = lax.optimization_barrier((arrived, mask))
    rows = GROUP * hidden
    loss, grads = pl.pallas_call(
        functools.partial(train_patch, scale),
        out_shape=(
            jax.ShapeDtypeStruct((planes, plane), jnp.float32),
            jax.ShapeDtypeStruct((hidden, hidden + bins), jnp.float32),
        ),
        in_specs=[vmem] * 5,
        out_specs=(pl.BlockSpec(memory_space=pl.ANY), vmem),
        scratch_shapes=[
            [pltpu.VMEM((taps, plane), jnp.bfloat16)] * (planes // GROUP),
            [[pltpu.VMEM((weights[1].shape[1], LANES), jnp.bfloat16)] * GROUP] * SLOTS,
            [[pltpu.VMEM((hidden, LANES), jnp.float32)] * GROUP] * SLOTS,
            [[pltpu.VMEM((bins, LANES), jnp.bfloat16)] * GROUP] * SLOTS,
            [[pltpu.VMEM((hidden, LANES), jnp.bfloat16)] * GROUP] * SLOTS,
            pltpu.VMEM((taps, rows), jnp.float32),
            pltpu.VMEM((hidden, bins), jnp.float32),
            pltpu.VMEM((hidden, 128), jnp.float32),
            pltpu.VMEM((bins, 128), jnp.float32),
            pltpu.VMEM((planes, plane), jnp.float32),
            pltpu.VMEM((planes, plane), jnp.float32),
            pltpu.VMEM((planes, plane), jnp.float32),
            pltpu.VMEM((rows // 128, taps, 128), jnp.float32),
            pltpu.SemaphoreType.DMA((planes // 8,)),
        ],
        compiler_params=pltpu.CompilerParams(vmem_limit_bytes=24 * 1024 * 1024),
        name="train_patch",
    )(arrived, patch_labels, *weights)
    shapes = (conv_weight.shape, (1, hidden), out_weight.shape, (1, bins))
    conv_grad, conv_bias_grad, out_grad, out_bias_grad = pl.pallas_call(
        unpack,
        out_shape=tuple(jax.ShapeDtypeStruct(shape, jnp.float32) for shape in shapes),
        in_specs=[vmem] * 3,
        out_specs=(vmem,) * 4,
        compiler_params=pltpu.CompilerParams(vmem_limit_bytes=8 * 1024 * 1024),
        name="unpack",
    )(*summed(grads), mask)
    return (
        loss.reshape(labels.shape),
        conv_grad,
        conv_bias_grad.reshape(conv_bias.shape),
        out_grad,
        out_bias_grad.reshape(out_bias.shape),
    )


def solution(mesh):
    placed = (P("dp", None, "sp", "sec"), P("dp", ("sec", "sp"), None, None), P(), P(), P(), P())
    return jax.shard_map(
        shards,
        mesh=mesh,
        in_specs=placed,
        out_specs=(P("dp", ("sec", "sp"), None, None), P(), P(), P(), P()),
        check_vma=False,
    )
```
